32 devices in a mesh: seg: 4 (over y, x), gx: 8 (over z, core).
Axes of the slice: x: 2, y: 2, z: 4, core: 2. Of those that a mesh axis runs over, the one named last changes fastest.
Arguments:
- start_states: float32 [4, 3, 24, 64, 384], P('seg', None, 'gx'), may hold values from -6 to 6
- base_flow: bfloat16 [4, 3, 3, 24, 64, 384], P('seg', None, None, 'gx'), may hold values from -3.5 to 3.5
Outputs:
- residual: float32 [4, 3, 24, 64, 384], P('seg', None, 'gx')
The draws below stay inside these ranges and needn't reach their ends.
All inputs are finite; a program needn't handle non-finite values.
Results may differ from the reference program's by a relative error of at most 0.0015.
Values may be sent and summed in bfloat16 or wider, within the bound.
A program may use at most 128 MiB of HBM per device.

```python
import jax
import jax.numpy as jnp

NY = 64
NZ = 384
STEPS = 3
SEGMENTS = 4
NX = 24


def shard_levels(rng, dims, shards, low, high):
    level, own = 1.0, jax.random.fold_in(rng, 6)
    for position, parts in shards:
        draws = jnp.exp(jax.random.uniform(jax.random.fold_in(own, position), (parts,), jnp.float32, low / len(shards), high / len(shards)))
        level = level * jnp.repeat(draws, dims[position] // parts).reshape([-1 if axis == position else 1 for axis in range(len(dims))])
    return level


def bell_draw(rng, dims, spread, most, pieces=(), kind=jnp.bfloat16):
    level = shard_levels(rng, dims, pieces, -0.22, 0.18) if pieces else 1.0
    values = jax.random.normal(rng, dims, jnp.float32) * spread * level
    return jnp.minimum(jnp.maximum(values, -most), most).astype(kind)


def setup_inputs(seed: int = 0) -> dict:
    streams_of = jax.random.split(jax.random.key(seed), 3)
    start_states = bell_draw(streams_of[0], (SEGMENTS, 3, NX, NY, NZ), 1.0, 6.0, ((0, 4), (2, 8)), jnp.float32)
    base_flow = bell_draw(streams_of[1], (SEGMENTS, STEPS, 3, NX, NY, NZ), 0.6, 3.5, ((0, 4), (3, 8)))
    return dict(start_states=start_states, base_flow=base_flow)


time_step = 0.3
viscosity = 0.45


def advance(q_ext, b_ext):
    centre = q_ext[:, 1:-1]
    base_c = b_ext[:, 1:-1]
    zero_row = jnp.zeros((3, centre.shape[1], 1, centre.shape[3]), jnp.float32)
    q_pad = jnp.concatenate([zero_row, centre, zero_row], axis=2)
    wall_sign = jnp.concatenate([jnp.ones((1, centre.shape[1], 1, centre.shape[3]), jnp.float32), jnp.zeros((2, centre.shape[1], 1, centre.shape[3]), jnp.float32)], axis=0)
    b_pad = jnp.concatenate([-wall_sign, base_c, wall_sign], axis=2)
    q_up = jnp.roll(centre, -1, 3)
    q_down = jnp.roll(centre, 1, 3)
    dq_x = (q_ext[:, 2:] - q_ext[:, :-2]) * 0.5
    dq_y = (q_pad[:, :, 2:] - q_pad[:, :, :-2]) * 0.5
    dq_z = (q_up - q_down) * 0.5
    db_x = (b_ext[:, 2:] - b_ext[:, :-2]) * 0.5
    db_y = (b_pad[:, :, 2:] - b_pad[:, :, :-2]) * 0.5
    db_z = (jnp.roll(base_c, -1, 3) - jnp.roll(base_c, 1, 3)) * 0.5
    lap = q_ext[:, 2:] + q_ext[:, :-2] + q_pad[:, :, 2:] + q_pad[:, :, :-2] + q_up + q_down - 6.0 * centre
    advect = base_c[0:1] * dq_x + base_c[1:2] * dq_y + base_c[2:3] * dq_z
    produce = centre[0:1] * db_x + centre[1:2] * db_y + centre[2:3] * db_z
    return centre + time_step * (viscosity * lap - advect - produce)


def wrapped(field, width):
    return jnp.concatenate([field[:, -width:], field, field[:, :width]], axis=1)


def mirror(field):
    shifted = jnp.roll(field, NX // 2, axis=1)
    flipped = jnp.roll(jnp.flip(shifted, 3), 1, 3)
    sign = jnp.concatenate([jnp.ones((2, 1, 1, 1), jnp.float32), -jnp.ones((1, 1, 1, 1), jnp.float32)], axis=0)
    return flipped * sign


def reference(start_states, base_flow):
    outputs = []
    for segment in range(SEGMENTS):
        state = start_states[segment]
        for step in range(STEPS):
            state = advance(wrapped(state, 1), wrapped(base_flow[segment, step].astype(jnp.float32), 1))
        if segment < SEGMENTS - 1:
            outputs.append(state - start_states[segment + 1])
        else:
            outputs.append(state - mirror(start_states[0]))
    return jnp.stack(outputs)
```

```python
import functools

import jax
import jax.numpy as jnp
from jax import lax
from jax.experimental import pallas as pl
from jax.experimental.pallas import tpu as pltpu
from jax.sharding import PartitionSpec as P

TIME_STEP = 0.3
VISCOSITY = 0.45
MESH = pl.DeviceIdType.MESH
ROWS = 16
PAD_Q = 8
PAD_B = 16
F32 = jnp.float32
BF16 = jnp.bfloat16


def encode(values):
    square = values * values
    fourth = square * square
    eighth = fourth * fourth
    return jnp.where(values < 0, -eighth, eighth).astype(BF16)


def decode(code):
    code = code.astype(F32)
    size = jnp.sqrt(jnp.sqrt(jnp.sqrt(jnp.abs(code))))
    return jnp.where(code < 0, -size, size)


def kernel(n_seg, n_gx, steps, nl, ny, nz, start_ref, base_ref, out_ref, q, b, hq, hb, sq, enc, ra, rb, tq, tgt,
           load_sem, qs_sem, qr_sem, bs_sem, br_sem, shift_sem, a_sem, ar_sem, b_sem, c_sem, cr_sem):
    seg = lax.axis_index("seg")
    gx = lax.axis_index("gx")
    last = n_seg - 1
    left, right = lax.rem(gx + n_gx - 1, n_gx), lax.rem(gx + 1, n_gx)
    across = lax.rem(gx + n_gx // 2, n_gx)
    relays = (0, 1, 2, last)
    quarter = ny // 4

    load_q = pltpu.make_async_copy(start_ref.at[0], q.at[0, :, :, pl.ds(PAD_Q, ny), :], load_sem.at[0])
    load_q.start()
    load_b = [
        pltpu.make_async_copy(base_ref.at[0, k], b.at[k, :, :, pl.ds(PAD_B, ny), :], load_sem.at[1 + k])
        for k in range(steps)
    ]
    for copy in load_b:
        copy.start()

    barrier = pltpu.get_barrier_semaphore()
    for other in (left, right, across):
        pl.semaphore_signal(barrier, inc=1, device_id={"gx": other}, device_id_type=MESH)
    for d in range(1, n_seg):
        pl.semaphore_signal(barrier, inc=1, device_id={"seg": lax.rem(seg + d, n_seg)}, device_id_type=MESH)

    def q_copy(k, side):
        return pltpu.make_async_remote_copy(
            src_ref=sq.at[k, side], dst_ref=hq.at[k, side], send_sem=qs_sem.at[k, side], recv_sem=qr_sem.at[k, side],
            device_id={"gx": right if side == 0 else left}, device_id_type=MESH)

    def b_copy(k, side):
        return pltpu.make_async_remote_copy(
            src_ref=base_ref.at[0, k, :, nl - 1 if side == 0 else 0], dst_ref=hb.at[k, side],
            send_sem=bs_sem.at[k, side], recv_sem=br_sem.at[k, side],
            device_id={"gx": right if side == 0 else left}, device_id_type=MESH)

    shift = pltpu.make_async_remote_copy(
        src_ref=start_ref.at[0], dst_ref=tgt, send_sem=shift_sem.at[0], recv_sem=shift_sem.at[1],
        device_id={"seg": lax.rem(seg + n_seg - 1, n_seg)}, device_id_type=MESH)

    def a_copy(j):
        return pltpu.make_async_remote_copy(
            src_ref=enc.at[j], dst_ref=ra, send_sem=a_sem.at[j], recv_sem=ar_sem.at[0],
            device_id={"seg": relays[j]}, device_id_type=MESH)

    def z_copy(source):
        return pltpu.make_async_remote_copy(
            src_ref=source, dst_ref=rb, send_sem=b_sem.at[0], recv_sem=b_sem.at[1],
            device_id={"gx": across}, device_id_type=MESH)

    def c_copy(j):
        return pltpu.make_async_remote_copy(
            src_ref=rb, dst_ref=tq.at[j], send_sem=c_sem.at[0], recv_sem=cr_sem.at[j],
            device_id={"seg": last}, device_id_type=MESH)

    q[:, :, :, 0:PAD_Q, :] = jnp.zeros((2, 3, nl, PAD_Q, nz), F32)
    q[:, :, :, PAD_Q + ny:, :] = jnp.zeros((2, 3, nl, PAD_Q, nz), F32)
    for c in range(3):
        wall = jnp.full((steps, nl, PAD_B, nz), 1.0 if c == 0 else 0.0, BF16)
        b[:, c, :, 0:PAD_B, :] = -wall
        b[:, c, :, PAD_B + ny:, :] = wall

    load_q.wait()
    for c in range(3):
        sq[0, 0, c] = q[0, c, nl - 1, PAD_Q:PAD_Q + ny, :].astype(BF16)
        sq[0, 1, c] = q[0, c, 0, PAD_Q:PAD_Q + ny, :].astype(BF16)

    pl.semaphore_wait(barrier, 3 + n_seg - 1)
    for side in range(2):
        q_copy(0, side).start()
        b_copy(0, side).start()

    @pl.when(seg == 0)
    def _():
        for j in range(4):
            for c in range(3):
                enc[j, c] = encode(q[0, c, :, PAD_Q + j * quarter:PAD_Q + (j + 1) * quarter, :])
        for j in range(1, 4):
            a_copy(j).start()

    @pl.when(seg > 0)
    def _():
        shift.start()

    def q_window(slot, c, x, at):
        window = q[slot, c, x, pl.ds(at, ROWS + 2 * PAD_Q), :]
        return window[PAD_Q:PAD_Q + ROWS], window

    def shifted(window, pad):
        size = window.shape[0]
        up = pltpu.roll(window, size - 1, 0)[pad:pad + ROWS]
        down = pltpu.roll(window, 1, 0)[pad:pad + ROWS]
        return up, down

    half = 0.5 * TIME_STEP
    diffuse = TIME_STEP * VISCOSITY

    def layer(k, x):
        slot = k % 2

        def chunk(r, carry):
            at = pl.multiple_of(r * ROWS, ROWS)
            here = pl.ds(at, ROWS)

            def q_side(c, side):
                neighbour = x + (-1 if side == 0 else 1)
                if 0 <= neighbour < nl:
                    return q[slot, c, neighbour, pl.ds(at + PAD_Q, ROWS), :]
                return hq[k, side, c, here, :].astype(F32)

            def b_side(c, side):
                neighbour = x + (-1 if side == 0 else 1)
                if 0 <= neighbour < nl:
                    return b[k, c, neighbour, pl.ds(at + PAD_B, ROWS), :].astype(F32)
                return hb[k, side, c, here, :].astype(F32)

            windows = [b[k, c, x, pl.ds(at, ROWS + 2 * PAD_B), :].astype(F32) for c in range(3)]
            carried = [half * window[PAD_B:PAD_B + ROWS] for window in windows]
            ahead = [diffuse - value for value in carried]
            behind = [diffuse + value for value in carried]
            centres = [q[slot, c, x, pl.ds(at + PAD_Q, ROWS), :] for c in range(3)]
            pushed = [half * value for value in centres]
            for c in range(3):
                centre, window = q_window(slot, c, x, at)
                up, down = shifted(window, PAD_Q)
                total = (1.0 - 6.0 * diffuse) * centre
                total += ahead[0] * q_side(c, 1) + behind[0] * q_side(c, 0)
                total += ahead[1] * up + behind[1] * down
                total += ahead[2] * pltpu.roll(centre, nz - 1, 1) + behind[2] * pltpu.roll(centre, 1, 1)
                total -= pushed[0] * (b_side(c, 1) - b_side(c, 0))
                base = windows[c][PAD_B - 8:PAD_B + ROWS + 8]
                up, down = shifted(base, 8)
                total -= pushed[1] * (up - down)
                base = windows[c][PAD_B:PAD_B + ROWS]
                total -= pushed[2] * (pltpu.roll(base, nz - 1, 1) - pltpu.roll(base, 1, 1))
                if k == steps - 1:
                    out_ref[0, c, x, here, :] = total - tgt[c, x, here, :]
                else:
                    q[1 - slot, c, x, pl.ds(at + PAD_Q, ROWS), :] = total
                    if x == nl - 1:
                        sq[k + 1, 0, c, here, :] = total.astype(BF16)
                    if x == 0:
                        sq[k + 1, 1, c, here, :] = total.astype(BF16)
            return carry

        lax.fori_loop(0, ny // ROWS, chunk, 0)

    def is_relay():
        flag = seg == 0
        for r in relays[1:]:
            flag = flag | (seg == r)
        return flag

    def finish_target():
        @pl.when(seg < last)
        def _():
            shift.wait_recv()

        @pl.when(seg == last)
        def _():
            z_copy(ra).wait_recv()
            for j in range(3):
                c_copy(j).wait_recv()
            row = lax.broadcasted_iota(jnp.int32, (nz, nz), 0)
            column = lax.broadcasted_iota(jnp.int32, (nz, nz), 1)
            flip = jnp.where((row + column == 0) | (row + column == nz), 1.0, 0.0).astype(BF16)
            for j in range(4):
                source = rb if j == 3 else tq.at[j]
                for c in range(3):
                    values = decode(source[c]).reshape(nl * quarter, nz)
                    high = values.astype(BF16)
                    low = (values - high.astype(F32)).astype(BF16)
                    flipped = jnp.dot(high, flip, preferred_element_type=F32)
                    flipped += jnp.dot(low, flip, preferred_element_type=F32)
                    if c == 2:
                        flipped = -flipped
                    tgt[c, :, j * quarter:(j + 1) * quarter, :] = flipped.reshape(nl, quarter, nz)

    for k in range(steps):
        load_b[k].wait()
        if k == steps - 1:
            finish_target()
            for x in range(1, nl - 1):
                layer(k, x)
        if k == 0:
            for x in range(1, nl - 1):
                layer(k, x)
            for side in range(2):
                b_copy(1, side).start()

            @pl.when(seg == 0)
            def _():
                z_copy(enc.at[0]).start()

            @pl.when((seg != 0) & is_relay())
            def _():
                a_copy(0).wait_recv()
                z_copy(ra).start()

        for side in range(2):
            q_copy(k, side).wait_recv()
            b_copy(k, side).wait_recv()
        layer(k, 0)
        layer(k, nl - 1)
        if k < steps - 1:
            for side in range(2):
                q_copy(k + 1, side).start()
            if k + 2 < steps:
                for side in range(2):
                    b_copy(k + 2, side).start()
        if 0 < k < steps - 1:
            for x in range(1, nl - 1):
                layer(k, x)

            @pl.when(is_relay() & (seg != last))
            def _():
                z_copy(ra).wait_recv()
                for j in range(3):
                    @pl.when(seg == relays[j])
                    def _():
                        c_copy(j).start()

    for k in range(steps):
        for side in range(2):
            q_copy(k, side).wait_send()
            b_copy(k, side).wait_send()

    @pl.when(seg > 0)
    def _():
        shift.wait_send()

    @pl.when(seg == 0)
    def _():
        for j in range(1, 4):
            a_copy(j).wait_send()

    @pl.when(is_relay())
    def _():
        z_copy(ra).wait_send()

    @pl.when(is_relay() & (seg != last))
    def _():
        c_copy(0).wait_send()


def local(n_seg, n_gx, start_states, base_flow):
    _, _, nl, ny, nz = start_states.shape
    steps = base_flow.shape[1]
    quarter = ny // 4
    dma = pltpu.SemaphoreType.DMA
    return pl.pallas_call(
        functools.partial(kernel, n_seg, n_gx, steps, nl, ny, nz),
        out_shape=jax.ShapeDtypeStruct(start_states.shape, F32),
        in_specs=[pl.BlockSpec(memory_space=pl.ANY)] * 2,
        out_specs=pl.BlockSpec(memory_space=pltpu.VMEM),
        scratch_shapes=[
            pltpu.VMEM((2, 3, nl, ny + 2 * PAD_Q, nz), F32),
            pltpu.VMEM((steps, 3, nl, ny + 2 * PAD_B, nz), BF16),
            pltpu.VMEM((steps, 2, 3, ny, nz), BF16),
            pltpu.VMEM((steps, 2, 3, ny, nz), BF16),
            pltpu.VMEM((steps, 2, 3, ny, nz), BF16),
            pltpu.VMEM((4, 3, nl, quarter, nz), BF16),
            pltpu.VMEM((3, nl, quarter, nz), BF16),
            pltpu.VMEM((3, nl, quarter, nz), BF16),
            pltpu.VMEM((3, 3, nl, quarter, nz), BF16),
            pltpu.VMEM((3, nl, ny, nz), F32),
            dma((1 + steps,)),
            dma((steps, 2)), dma((steps, 2)),
            dma((steps, 2)), dma((steps, 2)),
            dma((2,)),
            dma((4,)), dma((1,)),
            dma((2,)),
            dma((1,)), dma((3,)),
        ],
        compiler_params=pltpu.CompilerParams(
            collective_id=0, has_side_effects=True, vmem_limit_bytes=44 * 1024 * 1024),
        cost_estimate=pl.CostEstimate(flops=60_000_000, bytes_accessed=4_000_000, transcendentals=0),
    )(start_states, base_flow)


def solution(mesh):
    in_specs = (P("seg", None, "gx", None, None), P("seg", None, None, "gx", None, None))
    out_specs = P("seg", None, "gx", None, None)
    body = functools.partial(local, mesh.shape["seg"], mesh.shape["gx"])
    return jax.shard_map(body, mesh=mesh, in_specs=in_specs, out_specs=out_specs, check_vma=False)
```

```python
import functools

import jax
import jax.numpy as jnp
from jax import lax
from jax.experimental import pallas as pl
from jax.experimental.pallas import tpu as pltpu
from jax.sharding import PartitionSpec as P

TIME_STEP = 0.3
VISCOSITY = 0.45
MESH = pl.DeviceIdType.MESH
ROWS = 16
PAD_Q = 8
PAD_B = 16
F32 = jnp.float32
BF16 = jnp.bfloat16


def encode(values):
    square = values * values
    fourth = square * square
    eighth = fourth * fourth
    return jnp.where(values < 0, -eighth, eighth).astype(BF16)


def decode(code):
    code = code.astype(F32)
    size = jnp.sqrt(jnp.sqrt(jnp.sqrt(jnp.abs(code))))
    return jnp.where(code < 0, -size, size)


def kernel(n_seg, n_gx, steps, nl, ny, nz, start_ref, base_ref, out_ref, q, b, hq, hb, sq, enc, ra, rb, tq, tgt,
           load_sem, qs_sem, qr_sem, bs_sem, br_sem, shift_sem, a_sem, ar_sem, b_sem, c_sem, cr_sem):
    seg = lax.axis_index("seg")
    gx = lax.axis_index("gx")
    last = n_seg - 1
    left, right = lax.rem(gx + n_gx - 1, n_gx), lax.rem(gx + 1, n_gx)
    across = lax.rem(gx + n_gx // 2, n_gx)
    relays = (0, 1, 2, last)
    quarter = ny // 4

    load_q = pltpu.make_async_copy(start_ref.at[0], q.at[0, :, :, pl.ds(PAD_Q, ny), :], load_sem.at[0])
    load_q.start()
    load_b = [
        pltpu.make_async_copy(base_ref.at[0, k], b.at[k, :, :, pl.ds(PAD_B, ny), :], load_sem.at[1 + k])
        for k in range(steps)
    ]
    for copy in load_b:
        copy.start()

    barrier = pltpu.get_barrier_semaphore()
    for other in (left, right, across):
        pl.semaphore_signal(barrier, inc=1, device_id={"gx": other}, device_id_type=MESH)
    for d in range(1, n_seg):
        pl.semaphore_signal(barrier, inc=1, device_id={"seg": lax.rem(seg + d, n_seg)}, device_id_type=MESH)

    def q_copy(k, side):
        return pltpu.make_async_remote_copy(
            src_ref=sq.at[k, side], dst_ref=hq.at[k, side], send_sem=qs_sem.at[k, side], recv_sem=qr_sem.at[k, side],
            device_id={"gx": right if side == 0 else left}, device_id_type=MESH)

    def b_copy(k, side):
        return pltpu.make_async_remote_copy(
            src_ref=base_ref.at[0, k, :, nl - 1 if side == 0 else 0], dst_ref=hb.at[k, side],
            send_sem=bs_sem.at[k, side], recv_sem=br_sem.at[k, side],
            device_id={"gx": right if side == 0 else left}, device_id_type=MESH)

    shift = pltpu.make_async_remote_copy(
        src_ref=start_ref.at[0], dst_ref=tgt, send_sem=shift_sem.at[0], recv_sem=shift_sem.at[1],
        device_id={"seg": lax.rem(seg + n_seg - 1, n_seg)}, device_id_type=MESH)

    def a_copy(j):
        return pltpu.make_async_remote_copy(
            src_ref=enc.at[j], dst_ref=ra, send_sem=a_sem.at[j], recv_sem=ar_sem.at[0],
            device_id={"seg": relays[j]}, device_id_type=MESH)

    def z_copy(source):
        return pltpu.make_async_remote_copy(
            src_ref=source, dst_ref=rb, send_sem=b_sem.at[0], recv_sem=b_sem.at[1],
            device_id={"gx": across}, device_id_type=MESH)

    def c_copy(j):
        return pltpu.make_async_remote_copy(
            src_ref=rb, dst_ref=tq.at[j], send_sem=c_sem.at[0], recv_sem=cr_sem.at[j],
            device_id={"seg": last}, device_id_type=MESH)

    q[:, :, :, 0:PAD_Q, :] = jnp.zeros((2, 3, nl, PAD_Q, nz), F32)
    q[:, :, :, PAD_Q + ny:, :] = jnp.zeros((2, 3, nl, PAD_Q, nz), F32)
    for c in range(3):
        wall = jnp.full((steps, nl, PAD_B, nz), 1.0 if c == 0 else 0.0, BF16)
        b[:, c, :, 0:PAD_B, :] = -wall
        b[:, c, :, PAD_B + ny:, :] = wall

    pl.semaphore_wait(barrier, 3 + n_seg - 1)
    for side in range(2):
        b_copy(0, side).start()
    load_q.wait()
    for c in range(3):
        sq[0, 0, c] = q[0, c, nl - 1, PAD_Q:PAD_Q + ny, :].astype(BF16)
        sq[0, 1, c] = q[0, c, 0, PAD_Q:PAD_Q + ny, :].astype(BF16)

    for side in range(2):
        q_copy(0, side).start()

    @pl.when(seg == 0)
    def _():
        for j in range(4):
            for c in range(3):
                enc[j, c] = encode(q[0, c, :, PAD_Q + j * quarter:PAD_Q + (j + 1) * quarter, :])
        for j in range(1, 4):
            a_copy(j).start()

    @pl.when(seg > 0)
    def _():
        shift.start()

    def q_window(slot, c, x, at):
        window = q[slot, c, x, pl.ds(at, ROWS + 2 * PAD_Q), :]
        return window[PAD_Q:PAD_Q + ROWS], window

    def shifted(window, pad):
        size = window.shape[0]
        up = pltpu.roll(window, size - 1, 0)[pad:pad + ROWS]
        down = pltpu.roll(window, 1, 0)[pad:pad + ROWS]
        return up, down

    half = 0.5 * TIME_STEP
    diffuse = TIME_STEP * VISCOSITY

    def layer(k, x):
        slot = k % 2

        def chunk(r, carry):
            at = pl.multiple_of(r * ROWS, ROWS)
            here = pl.ds(at, ROWS)

            def q_side(c, side):
                neighbour = x + (-1 if side == 0 else 1)
                return q[slot, c, neighbour, pl.ds(at + PAD_Q, ROWS), :]

            def b_side(c, side):
                neighbour = x + (-1 if side == 0 else 1)
                return b[k, c, neighbour, pl.ds(at + PAD_B, ROWS), :].astype(F32)

            windows = [b[k, c, x, pl.ds(at, ROWS + 2 * PAD_B), :].astype(F32) for c in range(3)]
            carried = [half * window[PAD_B:PAD_B + ROWS] for window in windows]
            ahead = [diffuse - value for value in carried]
            behind = [diffuse + value for value in carried]
            centres = [q[slot, c, x, pl.ds(at + PAD_Q, ROWS), :] for c in range(3)]
            pushed = [half * value for value in centres]
            for c in range(3):
                centre, window = q_window(slot, c, x, at)
                up, down = shifted(window, PAD_Q)
                total = (1.0 - 6.0 * diffuse) * centre
                if x < nl - 1:
                    total += ahead[0] * q_side(c, 1) - pushed[0] * b_side(c, 1)
                if x > 0:
                    total += behind[0] * q_side(c, 0) + pushed[0] * b_side(c, 0)
                total += ahead[1] * up + behind[1] * down
                total += ahead[2] * pltpu.roll(centre, nz - 1, 1) + behind[2] * pltpu.roll(centre, 1, 1)
                base = windows[c][PAD_B - 8:PAD_B + ROWS + 8]
                up, down = shifted(base, 8)
                total -= pushed[1] * (up - down)
                base = windows[c][PAD_B:PAD_B + ROWS]
                total -= pushed[2] * (pltpu.roll(base, nz - 1, 1) - pltpu.roll(base, 1, 1))
                if k == steps - 1:
                    out_ref[0, c, x, here, :] = total
                else:
                    q[1 - slot, c, x, pl.ds(at + PAD_Q, ROWS), :] = total
            return carry

        lax.fori_loop(0, ny // ROWS, chunk, 0)

    def close(k, side):
        slot = k % 2
        x = 0 if side == 0 else nl - 1

        def chunk(r, carry):
            at = pl.multiple_of(r * ROWS, ROWS)
            here = pl.ds(at, ROWS)
            inner = pl.ds(at + PAD_Q, ROWS)
            carried = half * b[k, 0, x, pl.ds(at + PAD_B, ROWS), :].astype(F32)
            pushed = half * q[slot, 0, x, inner, :]
            weight = diffuse + carried if side == 0 else diffuse - carried
            for c in range(3):
                gained = weight * hq[k, side, c, here, :].astype(F32)
                pressed = pushed * hb[k, side, c, here, :].astype(F32)
                gained = gained + pressed if side == 0 else gained - pressed
                if k == steps - 1:
                    out_ref[0, c, x, here, :] += gained - tgt[c, x, here, :]
                else:
                    total = q[1 - slot, c, x, inner, :] + gained
                    q[1 - slot, c, x, inner, :] = total
                    sq[k + 1, 1 - side, c, here, :] = total.astype(BF16)
            return carry

        lax.fori_loop(0, ny // ROWS, chunk, 0)

    def is_relay():
        flag = seg == 0
        for r in relays[1:]:
            flag = flag | (seg == r)
        return flag

    def finish_target():
        @pl.when(seg < last)
        def _():
            shift.wait_recv()

        @pl.when(seg == last)
        def _():
            z_copy(ra).wait_recv()
            for j in range(3):
                c_copy(j).wait_recv()
            row = lax.broadcasted_iota(jnp.int32, (nz, nz), 0)
            column = lax.broadcasted_iota(jnp.int32, (nz, nz), 1)
            flip = jnp.where((row + column == 0) | (row + column == nz), 1.0, 0.0).astype(BF16)
            for j in range(4):
                source = rb if j == 3 else tq.at[j]
                for c in range(3):
                    values = decode(source[c]).reshape(nl * quarter, nz)
                    high = values.astype(BF16)
                    low = (values - high.astype(F32)).astype(BF16)
                    flipped = jnp.dot(high, flip, preferred_element_type=F32)
                    flipped += jnp.dot(low, flip, preferred_element_type=F32)
                    if c == 2:
                        flipped = -flipped
                    tgt[c, :, j * quarter:(j + 1) * quarter, :] = flipped.reshape(nl, quarter, nz)

    for k in range(steps):
        load_b[k].wait()
        for x in range(nl):
            layer(k, x)
        for side in range(2):
            q_copy(k, side).wait_send()
            b_copy(k, side).wait_send()
        if k + 1 < steps:
            for side in range(2):
                b_copy(k + 1, side).start()
        if k == 0:
            @pl.when(seg == 0)
            def _():
                z_copy(enc.at[0]).start()

            @pl.when((seg != 0) & is_relay())
            def _():
                a_copy(0).wait_recv()
                z_copy(ra).start()

        if k == steps - 1:
            finish_target()
            for x in range(1, nl - 1):
                for c in range(3):
                    out_ref[0, c, x] -= tgt[c, x]
        for side in range(2):
            q_copy(k, side).wait_recv()
            b_copy(k, side).wait_recv()
            close(k, side)
            if k < steps - 1:
                q_copy(k + 1, 1 - side).start()
        if k == steps - 2:
            @pl.when(is_relay() & (seg != last))
            def _():
                z_copy(ra).wait_recv()
                for j in range(3):
                    @pl.when(seg == relays[j])
                    def _():
                        c_copy(j).start()

    @pl.when(seg > 0)
    def _():
        shift.wait_send()

    @pl.when(seg == 0)
    def _():
        for j in range(1, 4):
            a_copy(j).wait_send()

    @pl.when(is_relay())
    def _():
        z_copy(ra).wait_send()

    @pl.when(is_relay() & (seg != last))
    def _():
        c_copy(0).wait_send()


def local(n_seg, n_gx, start_states, base_flow):
    _, _, nl, ny, nz = start_states.shape
    steps = base_flow.shape[1]
    quarter = ny // 4
    dma = pltpu.SemaphoreType.DMA
    return pl.pallas_call(
        functools.partial(kernel, n_seg, n_gx, steps, nl, ny, nz),
        out_shape=jax.ShapeDtypeStruct(start_states.shape, F32),
        in_specs=[pl.BlockSpec(memory_space=pltpu.HBM)] * 2,
        out_specs=pl.BlockSpec(memory_space=pltpu.VMEM),
        scratch_shapes=[
            pltpu.VMEM((2, 3, nl, ny + 2 * PAD_Q, nz), F32),
            pltpu.VMEM((steps, 3, nl, ny + 2 * PAD_B, nz), BF16),
            pltpu.VMEM((steps, 2, 3, ny, nz), BF16),
            pltpu.VMEM((steps, 2, 3, ny, nz), BF16),
            pltpu.VMEM((steps, 2, 3, ny, nz), BF16),
            pltpu.VMEM((4, 3, nl, quarter, nz), BF16),
            pltpu.VMEM((3, nl, quarter, nz), BF16),
            pltpu.VMEM((3, nl, quarter, nz), BF16),
            pltpu.VMEM((3, 3, nl, quarter, nz), BF16),
            pltpu.VMEM((3, nl, ny, nz), F32),
            dma((1 + steps,)),
            dma((steps, 2)), dma((steps, 2)),
            dma((steps, 2)), dma((steps, 2)),
            dma((2,)),
            dma((4,)), dma((1,)),
            dma((2,)),
            dma((1,)), dma((3,)),
        ],
        compiler_params=pltpu.CompilerParams(
            collective_id=0, has_side_effects=True, vmem_limit_bytes=60 * 1024 * 1024),
        cost_estimate=pl.CostEstimate(flops=60_000_000, bytes_accessed=4_000_000, transcendentals=0),
    )(start_states, base_flow)


def solution(mesh):
    in_specs = (P("seg", None, "gx", None, None), P("seg", None, None, "gx", None, None))
    out_specs = P("seg", None, "gx", None, None)
    body = functools.partial(local, mesh.shape["seg"], mesh.shape["gx"])
    return jax.shard_map(body, mesh=mesh, in_specs=in_specs, out_specs=out_specs, check_vma=False)
```

```python
import functools

import jax
import jax.numpy as jnp
from jax import lax
from jax.experimental import pallas as pl
from jax.experimental.pallas import tpu as pltpu
from jax.sharding import PartitionSpec as P

TIME_STEP = 0.3
VISCOSITY = 0.45
MESH = pl.DeviceIdType.MESH
ROWS = 16
EXCHANGED = (0,)
PAD_Q = 8
PAD_B = 16
F32 = jnp.float32
BF16 = jnp.bfloat16


def encode(values):
    square = values * values
    fourth = square * square
    eighth = fourth * fourth
    return jnp.where(values < 0, -eighth, eighth).astype(BF16)


def decode(code):
    code = code.astype(F32)
    size = jnp.sqrt(jnp.sqrt(jnp.sqrt(jnp.abs(code))))
    return jnp.where(code < 0, -size, size)


def kernel(n_seg, n_gx, steps, nl, ny, nz, start_ref, base_ref, out_ref, q, b, hq, hb, sq, enc, ra, rb, tq, tgt,
           load_sem, qs_sem, qr_sem, fs_sem, fr_sem, bs_sem, br_sem, shift_sem, a_sem, ar_sem, b_sem, c_sem, cr_sem):
    seg = lax.axis_index("seg")
    gx = lax.axis_index("gx")
    last = n_seg - 1
    left, right = lax.rem(gx + n_gx - 1, n_gx), lax.rem(gx + 1, n_gx)
    across = lax.rem(gx + n_gx // 2, n_gx)
    relays = (0, 1, 2, last)
    quarter = ny // 4

    load_q = pltpu.make_async_copy(start_ref.at[0], q.at[0, :, :, pl.ds(PAD_Q, ny), :], load_sem.at[0])
    load_q.start()
    load_b = [
        pltpu.make_async_copy(base_ref.at[0, k], b.at[k, :, :, pl.ds(PAD_B, ny), :], load_sem.at[1 + k])
        for k in range(steps)
    ]
    for copy in load_b:
        copy.start()

    barrier = pltpu.get_barrier_semaphore()
    for other in (left, right, across):
        pl.semaphore_signal(barrier, inc=1, device_id={"gx": other}, device_id_type=MESH)
    for d in range(1, n_seg):
        pl.semaphore_signal(barrier, inc=1, device_id={"seg": lax.rem(seg + d, n_seg)}, device_id_type=MESH)

    def comps(k):
        return pl.ds(0, 1 if k in EXCHANGED else 3)

    def q_copy(k, side):
        return pltpu.make_async_remote_copy(
            src_ref=sq.at[k, side, comps(k)], dst_ref=hq.at[k, side, comps(k)],
            send_sem=qs_sem.at[k, side], recv_sem=qr_sem.at[k, side],
            device_id={"gx": right if side == 0 else left}, device_id_type=MESH)

    def f_copy(k, side):
        return pltpu.make_async_remote_copy(
            src_ref=sq.at[k, side, pl.ds(1, 2)], dst_ref=hq.at[k, side, pl.ds(1, 2)],
            send_sem=fs_sem.at[k, side], recv_sem=fr_sem.at[k, side],
            device_id={"gx": right if side == 0 else left}, device_id_type=MESH)

    def b_copy(k, side):
        return pltpu.make_async_remote_copy(
            src_ref=base_ref.at[0, k, comps(k), nl - 1 if side == 0 else 0], dst_ref=hb.at[k, side, comps(k)],
            send_sem=bs_sem.at[k, side], recv_sem=br_sem.at[k, side],
            device_id={"gx": right if side == 0 else left}, device_id_type=MESH)

    shift = pltpu.make_async_remote_copy(
        src_ref=start_ref.at[0], dst_ref=tgt, send_sem=shift_sem.at[0], recv_sem=shift_sem.at[1],
        device_id={"seg": lax.rem(seg + n_seg - 1, n_seg)}, device_id_type=MESH)

    def a_copy(j):
        return pltpu.make_async_remote_copy(
            src_ref=enc.at[j], dst_ref=ra, send_sem=a_sem.at[j], recv_sem=ar_sem.at[0],
            device_id={"seg": relays[j]}, device_id_type=MESH)

    def z_copy(source):
        return pltpu.make_async_remote_copy(
            src_ref=source, dst_ref=rb, send_sem=b_sem.at[0], recv_sem=b_sem.at[1],
            device_id={"gx": across}, device_id_type=MESH)

    def c_copy(j):
        return pltpu.make_async_remote_copy(
            src_ref=rb, dst_ref=tq.at[j], send_sem=c_sem.at[0], recv_sem=cr_sem.at[j],
            device_id={"seg": last}, device_id_type=MESH)

    q[:, :, :, 0:PAD_Q, :] = jnp.zeros((2, 3, nl, PAD_Q, nz), F32)
    q[:, :, :, PAD_Q + ny:, :] = jnp.zeros((2, 3, nl, PAD_Q, nz), F32)
    for c in range(3):
        wall = jnp.full((steps, nl, PAD_B, nz), 1.0 if c == 0 else 0.0, BF16)
        b[:, c, :, 0:PAD_B, :] = -wall
        b[:, c, :, PAD_B + ny:, :] = wall

    load_q.wait()
    for c in range(1 if 0 in EXCHANGED else 3):
        sq[0, 0, c] = q[0, c, nl - 1, PAD_Q:PAD_Q + ny, :].astype(BF16)
        sq[0, 1, c] = q[0, c, 0, PAD_Q:PAD_Q + ny, :].astype(BF16)
    pl.semaphore_wait(barrier, 3 + n_seg - 1)
    for side in range(2):
        b_copy(0, side).start()
        q_copy(0, side).start()

    @pl.when(seg == 0)
    def _():
        for j in range(4):
            for c in range(3):
                enc[j, c] = encode(q[0, c, :, PAD_Q + j * quarter:PAD_Q + (j + 1) * quarter, :])
        for j in range(1, 4):
            a_copy(j).start()

    @pl.when(seg > 0)
    def _():
        shift.start()

    def q_window(slot, c, x, at):
        window = q[slot, c, x, pl.ds(at, ROWS + 2 * PAD_Q), :]
        return window[PAD_Q:PAD_Q + ROWS], window

    def shifted(window, pad):
        size = window.shape[0]
        up = pltpu.roll(window, size - 1, 0)[pad:pad + ROWS]
        down = pltpu.roll(window, 1, 0)[pad:pad + ROWS]
        return up, down

    half = 0.5 * TIME_STEP
    diffuse = TIME_STEP * VISCOSITY

    def layer(k, x):
        slot = k % 2

        def chunk(r, carry):
            at = pl.multiple_of(r * ROWS, ROWS)
            here = pl.ds(at, ROWS)

            def q_side(c, side):
                neighbour = x + (-1 if side == 0 else 1)
                return q[slot, c, neighbour, pl.ds(at + PAD_Q, ROWS), :]

            def b_side(c, side):
                neighbour = x + (-1 if side == 0 else 1)
                return b[k, c, neighbour, pl.ds(at + PAD_B, ROWS), :].astype(F32)

            windows = [b[k, c, x, pl.ds(at, ROWS + 2 * PAD_B), :].astype(F32) for c in range(3)]
            carried = [half * window[PAD_B:PAD_B + ROWS] for window in windows]
            ahead = [diffuse - value for value in carried]
            behind = [diffuse + value for value in carried]
            centres = [q[slot, c, x, pl.ds(at + PAD_Q, ROWS), :] for c in range(3)]
            pushed = [half * value for value in centres]
            for c in range(3):
                centre, window = q_window(slot, c, x, at)
                up, down = shifted(window, PAD_Q)
                total = (1.0 - 6.0 * diffuse) * centre
                if x < nl - 1:
                    total += ahead[0] * q_side(c, 1) - pushed[0] * b_side(c, 1)
                if x > 0:
                    total += behind[0] * q_side(c, 0) + pushed[0] * b_side(c, 0)
                total += ahead[1] * up + behind[1] * down
                total += ahead[2] * pltpu.roll(centre, nz - 1, 1) + behind[2] * pltpu.roll(centre, 1, 1)
                base = windows[c][PAD_B - 8:PAD_B + ROWS + 8]
                up, down = shifted(base, 8)
                total -= pushed[1] * (up - down)
                base = windows[c][PAD_B:PAD_B + ROWS]
                total -= pushed[2] * (pltpu.roll(base, nz - 1, 1) - pltpu.roll(base, 1, 1))
                if k == steps - 1:
                    out_ref[0, c, x, here, :] = total
                else:
                    q[1 - slot, c, x, pl.ds(at + PAD_Q, ROWS), :] = total
            return carry

        lax.fori_loop(0, ny // ROWS, chunk, 0)

    def close(k, side):
        slot = k % 2
        x = 0 if side == 0 else nl - 1

        def chunk(r, carry):
            at = pl.multiple_of(r * ROWS, ROWS)
            here = pl.ds(at, ROWS)
            inner = pl.ds(at + PAD_Q, ROWS)
            carried = half * b[k, 0, x, pl.ds(at + PAD_B, ROWS), :].astype(F32)
            pushed = half * q[slot, 0, x, inner, :]
            weight = diffuse + carried if side == 0 else diffuse - carried
            for c in range(3):
                gained = hq[k, side, c, here, :].astype(F32)
                if c == 0 or k not in EXCHANGED:
                    pressed = pushed * hb[k, side, c, here, :].astype(F32)
                    gained = weight * gained + pressed if side == 0 else weight * gained - pressed
                if k == steps - 1:
                    out_ref[0, c, x, here, :] += gained - tgt[c, x, here, :]
                else:
                    total = q[1 - slot, c, x, inner, :] + gained
                    q[1 - slot, c, x, inner, :] = total
                    if c == 0 or k + 1 not in EXCHANGED:
                        sq[k + 1, 1 - side, c, here, :] = total.astype(BF16)
            return carry

        lax.fori_loop(0, ny // ROWS, chunk, 0)

    def contribute(k, side):
        slot = k % 2
        x = 0 if side == 0 else nl - 1

        def chunk(r, carry):
            at = pl.multiple_of(r * ROWS, ROWS)
            here = pl.ds(at, ROWS)
            carried = half * hb[k, side, 0, here, :].astype(F32)
            pushed = half * hq[k, side, 0, here, :].astype(F32)
            for c in range(1, 3):
                mine = q[slot, c, x, pl.ds(at + PAD_Q, ROWS), :]
                base = b[k, c, x, pl.ds(at + PAD_B, ROWS), :].astype(F32)
                if side == 0:
                    share = (diffuse - carried) * mine - pushed * base
                else:
                    share = (diffuse + carried) * mine + pushed * base
                sq[k, 1 - side, c, here, :] = share.astype(BF16)
            return carry

        lax.fori_loop(0, ny // ROWS, chunk, 0)

    def is_relay():
        flag = seg == 0
        for r in relays[1:]:
            flag = flag | (seg == r)
        return flag

    def finish_target():
        @pl.when(seg < last)
        def _():
            shift.wait_recv()

        @pl.when(seg == last)
        def _():
            z_copy(ra).wait_recv()
            for j in range(3):
                c_copy(j).wait_recv()
            row = lax.broadcasted_iota(jnp.int32, (nz, nz), 0)
            column = lax.broadcasted_iota(jnp.int32, (nz, nz), 1)
            flip = jnp.where((row + column == 0) | (row + column == nz), 1.0, 0.0).astype(BF16)
            for j in range(4):
                source = rb if j == 3 else tq.at[j]
                for c in range(3):
                    values = decode(source[c]).reshape(nl * quarter, nz)
                    high = values.astype(BF16)
                    low = (values - high.astype(F32)).astype(BF16)
                    flipped = jnp.dot(high, flip, preferred_element_type=F32)
                    flipped += jnp.dot(low, flip, preferred_element_type=F32)
                    if c == 2:
                        flipped = -flipped
                    tgt[c, :, j * quarter:(j + 1) * quarter, :] = flipped.reshape(nl, quarter, nz)

    def start_relay():
        @pl.when(seg == 0)
        def _():
            z_copy(enc.at[0]).start()

        @pl.when((seg != 0) & is_relay())
        def _():
            a_copy(0).wait_recv()
            z_copy(ra).start()

    def sent(k):
        for side in range(2):
            q_copy(k, side).wait_send()
            b_copy(k, side).wait_send()
        if k + 1 < steps:
            for side in range(2):
                b_copy(k + 1, side).start()

    def arrived(k, side):
        q_copy(k, side).wait_recv()
        b_copy(k, side).wait_recv()

    for k in range(steps):
        load_b[k].wait()
        exchanged = k in EXCHANGED
        for x in range(nl):
            layer(k, x)
            if exchanged and x == nl - 2:
                sent(k)
        if exchanged:
            for side in range(2):
                arrived(k, side)
                contribute(k, side)
                f_copy(k, 1 - side).start()
        else:
            sent(k)
        if k == 0:
            if exchanged:
                for side in range(2):
                    f_copy(k, side).wait_send()
            start_relay()
        elif exchanged:
            for side in range(2):
                f_copy(k, side).wait_send()

        if k == steps - 1:
            finish_target()
            for x in range(1, nl - 1):
                for c in range(3):
                    out_ref[0, c, x] -= tgt[c, x]
        for side in range(2):
            if exchanged:
                f_copy(k, side).wait_recv()
            else:
                arrived(k, side)
            close(k, side)
            if k < steps - 1:
                q_copy(k + 1, 1 - side).start()
        if k == steps - 2:
            @pl.when(is_relay() & (seg != last))
            def _():
                z_copy(ra).wait_recv()
                for j in range(3):
                    @pl.when(seg == relays[j])
                    def _():
                        c_copy(j).start()

    @pl.when(seg > 0)
    def _():
        shift.wait_send()

    @pl.when(seg == 0)
    def _():
        for j in range(1, 4):
            a_copy(j).wait_send()

    @pl.when(is_relay())
    def _():
        z_copy(ra).wait_send()

    @pl.when(is_relay() & (seg != last))
    def _():
        c_copy(0).wait_send()


def local(n_seg, n_gx, start_states, base_flow):
    _, _, nl, ny, nz = start_states.shape
    steps = base_flow.shape[1]
    quarter = ny // 4
    dma = pltpu.SemaphoreType.DMA
    return pl.pallas_call(
        functools.partial(kernel, n_seg, n_gx, steps, nl, ny, nz),
        out_shape=jax.ShapeDtypeStruct(start_states.shape, F32),
        in_specs=[pl.BlockSpec(memory_space=pltpu.HBM)] * 2,
        out_specs=pl.BlockSpec(memory_space=pltpu.VMEM),
        scratch_shapes=[
            pltpu.VMEM((2, 3, nl, ny + 2 * PAD_Q, nz), F32),
            pltpu.VMEM((steps, 3, nl, ny + 2 * PAD_B, nz), BF16),
            pltpu.VMEM((steps, 2, 3, ny, nz), BF16),
            pltpu.VMEM((steps, 2, 3, ny, nz), BF16),
            pltpu.VMEM((steps, 2, 3, ny, nz), BF16),
            pltpu.VMEM((4, 3, nl, quarter, nz), BF16),
            pltpu.VMEM((3, nl, quarter, nz), BF16),
            pltpu.VMEM((3, nl, quarter, nz), BF16),
            pltpu.VMEM((3, 3, nl, quarter, nz), BF16),
            pltpu.VMEM((3, nl, ny, nz), F32),
            dma((1 + steps,)),
            dma((steps, 2)), dma((steps, 2)),
            dma((steps, 2)), dma((steps, 2)),
            dma((steps, 2)), dma((steps, 2)),
            dma((2,)),
            dma((4,)), dma((1,)),
            dma((2,)),
            dma((1,)), dma((3,)),
        ],
        compiler_params=pltpu.CompilerParams(
            collective_id=0, has_side_effects=True, vmem_limit_bytes=44 * 1024 * 1024),
        cost_estimate=pl.CostEstimate(flops=60_000_000, bytes_accessed=4_000_000, transcendentals=0),
    )(pltpu.with_memory_space_constraint(start_states, pltpu.HBM), pltpu.with_memory_space_constraint(base_flow, pltpu.HBM))


def solution(mesh):
    in_specs = (P("seg", None, "gx", None, None), P("seg", None, None, "gx", None, None))
    out_specs = P("seg", None, "gx", None, None)
    body = functools.partial(local, mesh.shape["seg"], mesh.shape["gx"])
    return jax.shard_map(body, mesh=mesh, in_specs=in_specs, out_specs=out_specs, check_vma=False)
```
